32 devices in a mesh: sens: 8 (over y, x, core), grp: 4 (over z).
Axes of the slice: x: 2, y: 2, z: 4, core: 2. Of those that a mesh axis runs over, the one named last changes fastest.
Arguments:
- histories: bfloat16 [256, 4096], P('sens', 'grp'), may hold values from -6 to 6
- bin_index: int32 [16], replicated, may hold values from 1 to 2047
- delays: int32 [256, 4096], P('sens'), may hold values from 0 to 4095
- map_adjoint: float32 [4096], replicated, may hold values from -48 to 48
Outputs:
- history_adjoint: bfloat16 [256, 4096], P('sens', 'grp')
The draws below stay inside these ranges and needn't reach their ends.
Inputs may be any that keep to these rules, and one draw needn't show every extreme that they name: `delays`: each delay is already reduced modulo 4096.
All inputs are finite; a program needn't handle non-finite values.
Results may differ from the reference program's by a relative error of at most 0.0059.
Values may be sent and summed in bfloat16 or wider, within the bound.
A program may use at most 64 MiB of HBM per device.

```python
import math
import jax
import jax.numpy as jnp
from jax import lax

NT = 4096
F = 16
G = 4096
SENSORS = 256


def with_ends(entries, stream_key, least, high):
    dims = entries.shape
    spot = [jax.random.randint(jax.random.fold_in(stream_key, axis), (), 0, dims[axis]) for axis in range(len(dims))]
    entries = entries.at[tuple(spot)].set(least)
    longest = dims.index(max(dims))
    spot[longest] = (spot[longest] + 1) % dims[longest]
    return entries.at[tuple(spot)].set(high)


def steps_of(rng, dims, cuts, smallest, high):
    level, own = 1.0, jax.random.fold_in(rng, 6)
    for dim, shards_of in cuts:
        steps = jnp.exp(jax.random.uniform(jax.random.fold_in(own, dim), (shards_of,), jnp.float32, smallest / len(cuts), high / len(cuts)))
        level = level * jnp.repeat(steps, dims[dim] // shards_of).reshape([-1 if axis == dim else 1 for axis in range(len(dims))])
    return level


def centred(stream_key, extent, scale, limit, cuts=(), kind=jnp.bfloat16):
    values = jax.random.normal(stream_key, extent, jnp.float32) * scale
    if len(cuts) > 0:
        values = steps_of(stream_key, extent, cuts, -0.22, 0.18) * values
    return jnp.clip(values, min=-limit, max=limit).astype(kind)


def setup_inputs(seed: int = 0) -> dict:
    streams_of = jax.random.split(jax.random.key(seed), 5)
    histories = centred(streams_of[0], (SENSORS, NT), 1.0, 6.0, ((0, 8), (1, 4)))
    bin_index = with_ends(jax.random.randint(streams_of[1], (F,), 1, NT // 2), jax.random.fold_in(streams_of[1], 1), 1, (NT // 2) - 1).astype(jnp.int32)
    delays = with_ends(jax.random.randint(streams_of[2], (SENSORS, G), 0, NT), jax.random.fold_in(streams_of[2], 1), 0, NT - 1).astype(jnp.int32)
    map_adjoint = centred(streams_of[3], (G,), 8.0, 48.0, (), jnp.float32)
    return {"histories": histories, "bin_index": bin_index, "delays": delays, "map_adjoint": map_adjoint}


two_pi = 2.0 * math.pi

def plain_transform(length, bin_index):
    sample_times = jnp.arange(length, dtype=jnp.int32)
    phase_index = sample_times[:, None] * bin_index[None, :] % length
    phase_angle = phase_index.astype(jnp.float32) * (two_pi / length)
    factor = 1.0 / math.sqrt(length)
    cosine = jnp.cos(phase_angle) * factor
    sine_part = -jnp.sin(phase_angle) * factor
    return jnp.concatenate([cosine, sine_part], 1).astype(jnp.bfloat16)

def angles(bin_index, delay_block, length):
    phase_index = bin_index[:, None, None] * delay_block[None, :, :] % length
    return phase_index.astype(jnp.float32) * (two_pi / length)

def steer_forward(real_part, imag_part, delays, bin_index, length, steer_scale, block_cap):
    scan_count = delays.shape[1]
    block_size = math.gcd(scan_count, block_cap)
    real_trans = real_part.T
    imag_trans = imag_part.T
    highest = lax.Precision.HIGHEST

    def one_block(block_index):
        delay_block = lax.dynamic_slice_in_dim(delays, block_index * block_size, block_size, 1)
        phase_angle = angles(bin_index, delay_block, length)
        cosine = jnp.cos(phase_angle)
        sine_part = jnp.sin(phase_angle)
        steer_real = jnp.einsum('fs,fsg->fg', real_trans, cosine, precision=highest) - jnp.einsum('fs,fsg->fg', imag_trans, sine_part, precision=highest)
        steer_imag = jnp.einsum('fs,fsg->fg', real_trans, sine_part, precision=highest) + jnp.einsum('fs,fsg->fg', imag_trans, cosine, precision=highest)
        return (steer_real * steer_scale, steer_imag * steer_scale)
    blocks_real, blocks_imag = lax.map(one_block, jnp.arange(scan_count // block_size, dtype=jnp.int32))
    bin_count = bin_index.shape[0]
    return (blocks_real.transpose(1, 0, 2).reshape(bin_count, scan_count), blocks_imag.transpose(1, 0, 2).reshape(bin_count, scan_count))

def steer_back(bar_real, bar_imag, delays, bin_index, length, steer_scale, block_cap):
    scan_count = delays.shape[1]
    block_size = math.gcd(scan_count, block_cap)
    highest = lax.Precision.HIGHEST

    def add_block(block_index, totals):
        delay_block = lax.dynamic_slice_in_dim(delays, block_index * block_size, block_size, 1)
        block_real = lax.dynamic_slice_in_dim(bar_real, block_index * block_size, block_size, 1)
        block_imag = lax.dynamic_slice_in_dim(bar_imag, block_index * block_size, block_size, 1)
        phase_angle = angles(bin_index, delay_block, length)
        cosine = jnp.cos(phase_angle)
        sine_part = jnp.sin(phase_angle)
        back_real = jnp.einsum('fg,fsg->fs', block_real, cosine, precision=highest) + jnp.einsum('fg,fsg->fs', block_imag, sine_part, precision=highest)
        back_imag = jnp.einsum('fg,fsg->fs', block_imag, cosine, precision=highest) - jnp.einsum('fg,fsg->fs', block_real, sine_part, precision=highest)
        return (totals[0] + back_real, totals[1] + back_imag)
    zeros_start = jnp.zeros((bin_index.shape[0], delays.shape[0]), jnp.float32)
    total_real, total_imag = lax.fori_loop(0, scan_count // block_size, add_block, (zeros_start, zeros_start))
    return (total_real.T * steer_scale, total_imag.T * steer_scale)

def reference(histories, bin_index, delays, map_adjoint):
    transform = plain_transform(NT, bin_index)
    spectra = jnp.dot(histories, transform, preferred_element_type=jnp.float32)
    real_part = spectra[:, :F]
    imag_part = spectra[:, F:]
    steer_scale = 1.0 / math.sqrt(SENSORS)
    steer_real, steer_imag = steer_forward(real_part, imag_part, delays, bin_index, NT, steer_scale, 32)
    weight = 2.0 * map_adjoint[None, :]
    back_real, back_imag = steer_back(weight * steer_real, weight * steer_imag, delays, bin_index, NT, steer_scale, 32)
    adjoint = jnp.concatenate([back_real, back_imag], 1).astype(jnp.bfloat16)
    return jnp.dot(adjoint, transform.T, preferred_element_type=jnp.float32).astype(jnp.bfloat16)
```

```python
import functools
import math

import jax
import jax.numpy as jnp
from jax import lax
from jax.experimental import pallas as pl
from jax.experimental.pallas import tpu as pltpu
from jax.sharding import PartitionSpec as P

NT = 4096


two_pi = 2.0 * math.pi


def grouped_transform(first_sample, sample_count, bin_index, length, groups):
    sample_times = first_sample + lax.iota(jnp.int32, sample_count)
    phase_index = sample_times[:, None] * bin_index[None, :] % length
    phase_angle = phase_index.astype(jnp.float32) * (two_pi / length)
    factor = 1.0 / math.sqrt(length)
    bin_width = bin_index.shape[0] // groups
    cosine = (jnp.cos(phase_angle) * factor).reshape(sample_count, groups, 1, bin_width)
    sine_part = (-jnp.sin(phase_angle) * factor).reshape(sample_count, groups, 1, bin_width)
    joined_parts = jnp.concatenate([cosine, sine_part], 2)
    return joined_parts.reshape(sample_count, 2 * bin_index.shape[0]).astype(jnp.bfloat16)


def angles(bin_index, delay_block, length):
    phase_index = bin_index[:, None, None] * delay_block[None, :, :] % length
    return phase_index.astype(jnp.float32) * (two_pi / length)


def steer_forward(real_part, imag_part, delays, bin_index, length, steer_scale):
    scan_count = delays.shape[1]
    block_size = math.gcd(scan_count, 512)
    real_trans = real_part.T
    imag_trans = imag_part.T
    highest = lax.Precision.HIGHEST

    def one_block(block_index):
        delay_block = lax.dynamic_slice_in_dim(delays, block_index * block_size, block_size, 1)
        phase_angle = angles(bin_index, delay_block, length)
        cosine = jnp.cos(phase_angle)
        sine_part = jnp.sin(phase_angle)
        steer_real = jnp.einsum("fs,fsg->fg", real_trans, cosine, precision=highest) - jnp.einsum(
            "fs,fsg->fg", imag_trans, sine_part, precision=highest
        )
        steer_imag = jnp.einsum(
            "fs,fsg->fg", real_trans, sine_part, precision=highest
        ) + jnp.einsum("fs,fsg->fg", imag_trans, cosine, precision=highest)
        return (steer_real * steer_scale, steer_imag * steer_scale)

    blocks_real, blocks_imag = lax.map(
        one_block, jnp.arange(scan_count // block_size, dtype=jnp.int32)
    )
    bin_count = bin_index.shape[0]
    return (
        blocks_real.transpose(1, 0, 2).reshape(bin_count, scan_count),
        blocks_imag.transpose(1, 0, 2).reshape(bin_count, scan_count),
    )


def steer_back(bar_real, bar_imag, delays, bin_index, length, steer_scale):
    scan_count = delays.shape[1]
    block_size = math.gcd(scan_count, 512)
    highest = lax.Precision.HIGHEST

    def add_block(block_index, totals):
        delay_block = lax.dynamic_slice_in_dim(delays, block_index * block_size, block_size, 1)
        block_real = lax.dynamic_slice_in_dim(bar_real, block_index * block_size, block_size, 1)
        block_imag = lax.dynamic_slice_in_dim(bar_imag, block_index * block_size, block_size, 1)
        phase_angle = angles(bin_index, delay_block, length)
        cosine = jnp.cos(phase_angle)
        sine_part = jnp.sin(phase_angle)
        back_real = jnp.einsum("fg,fsg->fs", block_real, cosine, precision=highest) + jnp.einsum(
            "fg,fsg->fs", block_imag, sine_part, precision=highest
        )
        back_imag = jnp.einsum("fg,fsg->fs", block_imag, cosine, precision=highest) - jnp.einsum(
            "fg,fsg->fs", block_real, sine_part, precision=highest
        )
        return (totals[0] + back_real, totals[1] + back_imag)

    zeros_start = jnp.zeros((bin_index.shape[0], delays.shape[0]), jnp.float32)
    total_real, total_imag = lax.fori_loop(
        0, scan_count // block_size, add_block, (zeros_start, zeros_start)
    )
    return (total_real.T * steer_scale, total_imag.T * steer_scale)


def on_device_plain(histories, bin_index, delays, map_adjoint):
    groups = lax.axis_size("grp")
    sensors = delays.shape[0] * lax.axis_size("sens")
    steer_scale = 1.0 / math.sqrt(sensors)
    block_rows = histories.shape[1]
    position = lax.axis_index("grp")
    weight = 2.0 * map_adjoint[None, :]
    transform = grouped_transform(position * block_rows, block_rows, bin_index, NT, groups)
    partial_value = jnp.dot(histories, transform, preferred_element_type=jnp.float32)
    spectra = lax.psum_scatter(partial_value, "grp", scatter_dimension=1, tiled=True)
    bin_width = bin_index.shape[0] // groups
    own_bins = lax.dynamic_slice_in_dim(bin_index, position * bin_width, bin_width, 0)
    real_part = spectra[:, :bin_width]
    imag_part = spectra[:, bin_width:]
    steer_real, steer_imag = steer_forward(real_part, imag_part, delays, own_bins, NT, steer_scale)
    steer_real, steer_imag = lax.psum((steer_real, steer_imag), "sens")
    back_real, back_imag = steer_back(
        weight * steer_real, weight * steer_imag, delays, own_bins, NT, steer_scale
    )
    adjoint = jnp.concatenate([back_real, back_imag], 1).astype(jnp.bfloat16)
    result = lax.dot_general(
        lax.all_gather(adjoint, "grp", axis=1, tiled=True),
        transform,
        (((1,), (1,)), ((), ())),
        preferred_element_type=jnp.float32,
    )
    return result.astype(jnp.bfloat16)


MESH = pl.DeviceIdType.MESH
COS_T = (0.9999992216, -19.73898252, 64.92872662, -85.27239701, 58.79403871, -21.07678212)
SIN_T = (6.283055799, -41.33121431, 81.36681529, -74.47800454, 32.78140079)
COS_W = (
    0.9999999892,
    -19.73920453,
    64.93911898,
    -85.45016555,
    60.16783172,
    -25.96831327,
    6.529610372,
)
CHUNK = 256


def horner(coefficients, u):
    value = coefficients[-1] * u + coefficients[-2]
    for coefficient in coefficients[-3::-1]:
        value = value * u + coefficient
    return value


def wrapped(turns):
    return turns - jnp.round(turns)


def kernel(
    ns,
    ng,
    scale,
    bins_ref,
    map_ref,
    hist_hbm,
    delays_hbm,
    out_ref,
    hist,
    delays,
    wave,
    steer,
    spec_out,
    spec_in,
    part_out,
    part_in,
    bar_out,
    bar_in,
    adj,
    local_sem,
    spec_send,
    spec_recv,
    part_send,
    part_recv,
    bar_send,
    bar_recv,
    adj_send,
    adj_recv,
):
    f32, bf16 = jnp.float32, jnp.bfloat16
    sens, grp = lax.axis_index("sens"), lax.axis_index("grp")
    rows, times = hist.shape
    points = delays.shape[1]
    width = points // ns
    half = width // 2
    blocks = wave.shape[0] // 16
    length = times * ng

    def sens_at(offset):
        return lax.rem(sens + offset, ns)

    def grp_at(offset):
        return lax.rem(grp + offset, ng)

    hist_copy = pltpu.make_async_copy(hist_hbm, hist, local_sem.at[0])
    delays_copy = pltpu.make_async_copy(delays_hbm, delays, local_sem.at[1])
    hist_copy.start()
    delays_copy.start()
    barrier = pltpu.get_barrier_semaphore()
    for k in range(1, ns):
        pl.semaphore_signal(barrier, inc=1, device_id={"sens": sens_at(k)}, device_id_type=MESH)
    for k in range(1, ng):
        pl.semaphore_signal(barrier, inc=1, device_id={"grp": grp_at(k)}, device_id_type=MESH)

    row8 = lax.broadcasted_iota(jnp.int32, (8, times), 0)
    sample = (grp * times + lax.broadcasted_iota(jnp.int32, (8, times), 1)).astype(f32)
    lower = row8 >= 4
    which = lax.rem(row8, 4)
    for j in range(blocks):
        b = [bins_ref[4 * j + i].astype(f32) * (1.0 / length) for i in range(4)]
        column = jnp.where(
            which == 0, b[0], jnp.where(which == 1, b[1], jnp.where(which == 2, b[2], b[3]))
        )
        r = wrapped(sample * column + jnp.where(lower, 0.25, 0.0))
        values = horner(COS_W, r * r) * (1.0 / math.sqrt(length))
        wave[16 * j : 16 * j + 16, :] = jnp.concatenate(
            [values, jnp.zeros((8, times), f32)], 0
        ).astype(bf16)

    hist_copy.wait()
    partial_spectra = lax.dot_general(
        wave[...], hist[...], (((1,), (1,)), ((), ())), preferred_element_type=f32
    )
    spec_out[...] = jnp.zeros(spec_out.shape, f32)
    for j in range(ng):
        spec_out[j, :, 0:rows] = partial_spectra[16 * j : 16 * j + 8, :]
    pl.semaphore_wait(barrier, ns - 1 + ng - 1)

    spec_copies = []
    for k in range(1, ng):
        copy = pltpu.make_async_remote_copy(
            src_ref=spec_out.at[grp_at(k)],
            dst_ref=spec_in.at[k - 1],
            send_sem=spec_send.at[k - 1],
            recv_sem=spec_recv.at[k - 1],
            device_id={"grp": grp_at(k)},
            device_id_type=MESH,
        )
        copy.start()
        spec_copies.append(copy)

    delays_copy.wait()
    own_bins = [bins_ref[4 * grp + i].astype(f32) * (1.0 / length) for i in range(4)]

    def steer_chunk(index, carry):
        at = pl.ds(pl.multiple_of(index * CHUNK, CHUNK), CHUNK)
        delay = delays[:, at].astype(f32)
        for i in range(4):
            r = wrapped(delay * own_bins[i])
            u = r * r
            steer[64 * i : 64 * i + 32, at] = horner(COS_T, u).astype(bf16)
            steer[64 * i + 32 : 64 * i + 64, at] = (horner(SIN_T, u) * r).astype(bf16)
        return carry

    lax.fori_loop(0, points // CHUNK, steer_chunk, 0)

    sign = jnp.where(lax.broadcasted_iota(jnp.int32, (8, 128), 0) < 4, -1.0, 1.0).astype(f32)
    own_block = lax.rem(lax.broadcasted_iota(jnp.int32, (8, 256), 0), 4) == (
        lax.broadcasted_iota(jnp.int32, (8, 256), 1) // 64
    )
    total = spec_out[grp]
    for k in range(1, ng):
        spec_copies[k - 1].wait_recv()
        total = total + spec_in[k - 1]
    both = total + pltpu.roll(sign * pltpu.roll(total, 4, 0), 32, 1)
    both = both + pltpu.roll(both, 64, 1)
    spread = jnp.where(own_block, jnp.concatenate([both, both], 1), 0.0)
    high = spread.astype(bf16).astype(f32)
    lhs = jnp.concatenate([high, spread - high], 0).astype(bf16)

    def steered_part(owner):
        at = pl.ds(pl.multiple_of(owner * width, width), width)
        product = jnp.dot(lhs, steer[:, at], preferred_element_type=f32)
        product = product[0:8] + product[8:16]
        return jnp.concatenate([product[:, 0:half], product[:, half:width]], 0)

    part_copies = []
    for k in range(1, ns):
        part_out[k - 1] = steered_part(sens_at(k)).astype(bf16)
        copy = pltpu.make_async_remote_copy(
            src_ref=part_out.at[k - 1],
            dst_ref=part_in.at[k - 1],
            send_sem=part_send.at[k - 1],
            recv_sem=part_recv.at[k - 1],
            device_id={"sens": sens_at(k)},
            device_id_type=MESH,
        )
        copy.start()
        part_copies.append(copy)
    total = steered_part(sens)
    first = map_ref[:, pl.ds(pl.multiple_of(sens * width, width), half)]
    second = map_ref[:, pl.ds(pl.multiple_of(sens * width + half, half), half)]
    weight = (2.0 * scale * scale) * jnp.concatenate(
        [jnp.broadcast_to(first, (8, half)), jnp.broadcast_to(second, (8, half))], 0
    )
    for k in range(1, ns):
        part_copies[k - 1].wait_recv()
        total = total + part_in[k - 1].astype(f32)
    bar = (weight * total).astype(bf16)
    bar_out[...] = bar

    bar_copies = []
    for k in range(1, ns):
        copy = pltpu.make_async_remote_copy(
            src_ref=bar_out,
            dst_ref=bar_in.at[k - 1],
            send_sem=bar_send.at[k - 1],
            recv_sem=bar_recv.at[k - 1],
            device_id={"sens": sens_at(k)},
            device_id_type=MESH,
        )
        copy.start()
        bar_copies.append(copy)

    def back_part(values, owner):
        sides = []
        for side in range(2):
            at = pl.ds(pl.multiple_of(owner * width + side * half, half), half)
            sides.append(
                lax.dot_general(
                    values,
                    steer[:, at],
                    (((1,), (1,)), ((), ())),
                    preferred_element_type=f32,
                )
            )
        return sides[0][0:8] + sides[1][8:16]

    back = back_part(bar, sens)
    for k in range(1, ns):
        bar_copies[k - 1].wait_recv()
        back = back + back_part(bar_in[k - 1], sens_at(ns - k))
    back = jnp.where(own_block, back, 0.0)
    back = back[:, 0:128] + back[:, 128:256]
    back = back + pltpu.roll(back, 64, 1)
    back = back - sign * pltpu.roll(pltpu.roll(back, 4, 0), 96, 1)
    own_rows = jnp.concatenate([back, jnp.zeros((8, 128), f32)], 0).astype(bf16)
    adj[grp] = own_rows

    adj_copies = []
    for k in range(1, ng):
        copy = pltpu.make_async_remote_copy(
            src_ref=adj.at[grp],
            dst_ref=adj.at[grp],
            send_sem=adj_send.at[k - 1],
            recv_sem=adj_recv.at[k - 1],
            device_id={"grp": grp_at(k)},
            device_id_type=MESH,
        )
        copy.start()
        adj_copies.append(copy)
    for copy in adj_copies:
        copy.wait_recv()
    gathered = jnp.concatenate([adj[j] for j in range(ng)], 0)
    out_ref[...] = lax.dot_general(
        gathered[:, 0:rows], wave[...], (((0,), (0,)), ((), ())), preferred_element_type=f32
    ).astype(bf16)
    for copy in spec_copies + part_copies + bar_copies + adj_copies:
        copy.wait_send()


def on_device_fused(ns, ng, histories, bin_index, delays, map_adjoint):
    rows, times = histories.shape
    points = delays.shape[1]
    half = points // ns // 2
    dma = pltpu.SemaphoreType.DMA
    vmem = pltpu.VMEM
    return pl.pallas_call(
        functools.partial(kernel, ns, ng, 1.0 / math.sqrt(rows * ns)),
        out_shape=jax.ShapeDtypeStruct((rows, times), jnp.bfloat16),
        in_specs=[
            pl.BlockSpec(memory_space=pltpu.SMEM),
            pl.BlockSpec(memory_space=pltpu.VMEM),
            pl.BlockSpec(memory_space=pl.ANY),
            pl.BlockSpec(memory_space=pl.ANY),
        ],
        out_specs=pl.BlockSpec(memory_space=pltpu.VMEM),
        scratch_shapes=[
            vmem((rows, times), jnp.bfloat16),
            vmem((rows, points), jnp.int32),
            vmem((16 * ng, times), jnp.bfloat16),
            vmem((256, points), jnp.bfloat16),
            vmem((ng, 8, 128), jnp.float32),
            vmem((ng - 1, 8, 128), jnp.float32),
            vmem((ns - 1, 16, half), jnp.bfloat16),
            vmem((ns - 1, 16, half), jnp.bfloat16),
            vmem((16, half), jnp.bfloat16),
            vmem((ns - 1, 16, half), jnp.bfloat16),
            vmem((ng, 16, 128), jnp.bfloat16),
            dma((2,)),
            dma((ng - 1,)),
            dma((ng - 1,)),
            dma((ns - 1,)),
            dma((ns - 1,)),
            dma((ns - 1,)),
            dma((ns - 1,)),
            dma((ng - 1,)),
            dma((ng - 1,)),
        ],
        compiler_params=pltpu.CompilerParams(
            collective_id=0, has_side_effects=True, vmem_limit_bytes=32 * 1024 * 1024
        ),
    )(bin_index, map_adjoint.reshape(1, points), histories, delays)


def solution(mesh):
    ns, ng = mesh.shape["sens"], mesh.shape["grp"]
    placed = (P("sens", "grp"), P(), P("sens", None), P())

    def on_device(histories, bin_index, delays, map_adjoint):
        rows, points = delays.shape
        fits = (
            rows == 32
            and bin_index.shape[0] == 4 * ng
            and points % (256 * ns) == 0
            and histories.shape[1] * ng == NT
        )
        if fits:
            return on_device_fused(ns, ng, histories, bin_index, delays, map_adjoint)
        return on_device_plain(histories, bin_index, delays, map_adjoint)

    return jax.shard_map(
        on_device, mesh=mesh, in_specs=placed, out_specs=P("sens", "grp"), check_vma=False
    )
```

```python
import functools
import math

import jax
import jax.numpy as jnp
from jax import lax
from jax.experimental import pallas as pl
from jax.experimental.pallas import tpu as pltpu
from jax.sharding import PartitionSpec as P

NT = 4096


two_pi = 2.0 * math.pi


def grouped_transform(first_sample, sample_count, bin_index, length, groups):
    sample_times = first_sample + lax.iota(jnp.int32, sample_count)
    phase_index = sample_times[:, None] * bin_index[None, :] % length
    phase_angle = phase_index.astype(jnp.float32) * (two_pi / length)
    factor = 1.0 / math.sqrt(length)
    bin_width = bin_index.shape[0] // groups
    cosine = (jnp.cos(phase_angle) * factor).reshape(sample_count, groups, 1, bin_width)
    sine_part = (-jnp.sin(phase_angle) * factor).reshape(sample_count, groups, 1, bin_width)
    joined_parts = jnp.concatenate([cosine, sine_part], 2)
    return joined_parts.reshape(sample_count, 2 * bin_index.shape[0]).astype(jnp.bfloat16)


def angles(bin_index, delay_block, length):
    phase_index = bin_index[:, None, None] * delay_block[None, :, :] % length
    return phase_index.astype(jnp.float32) * (two_pi / length)


def steer_forward(real_part, imag_part, delays, bin_index, length, steer_scale):
    scan_count = delays.shape[1]
    block_size = math.gcd(scan_count, 512)
    real_trans = real_part.T
    imag_trans = imag_part.T
    highest = lax.Precision.HIGHEST

    def one_block(block_index):
        delay_block = lax.dynamic_slice_in_dim(delays, block_index * block_size, block_size, 1)
        phase_angle = angles(bin_index, delay_block, length)
        cosine = jnp.cos(phase_angle)
        sine_part = jnp.sin(phase_angle)
        steer_real = jnp.einsum("fs,fsg->fg", real_trans, cosine, precision=highest) - jnp.einsum(
            "fs,fsg->fg", imag_trans, sine_part, precision=highest
        )
        steer_imag = jnp.einsum(
            "fs,fsg->fg", real_trans, sine_part, precision=highest
        ) + jnp.einsum("fs,fsg->fg", imag_trans, cosine, precision=highest)
        return (steer_real * steer_scale, steer_imag * steer_scale)

    blocks_real, blocks_imag = lax.map(
        one_block, jnp.arange(scan_count // block_size, dtype=jnp.int32)
    )
    bin_count = bin_index.shape[0]
    return (
        blocks_real.transpose(1, 0, 2).reshape(bin_count, scan_count),
        blocks_imag.transpose(1, 0, 2).reshape(bin_count, scan_count),
    )


def steer_back(bar_real, bar_imag, delays, bin_index, length, steer_scale):
    scan_count = delays.shape[1]
    block_size = math.gcd(scan_count, 512)
    highest = lax.Precision.HIGHEST

    def add_block(block_index, totals):
        delay_block = lax.dynamic_slice_in_dim(delays, block_index * block_size, block_size, 1)
        block_real = lax.dynamic_slice_in_dim(bar_real, block_index * block_size, block_size, 1)
        block_imag = lax.dynamic_slice_in_dim(bar_imag, block_index * block_size, block_size, 1)
        phase_angle = angles(bin_index, delay_block, length)
        cosine = jnp.cos(phase_angle)
        sine_part = jnp.sin(phase_angle)
        back_real = jnp.einsum("fg,fsg->fs", block_real, cosine, precision=highest) + jnp.einsum(
            "fg,fsg->fs", block_imag, sine_part, precision=highest
        )
        back_imag = jnp.einsum("fg,fsg->fs", block_imag, cosine, precision=highest) - jnp.einsum(
            "fg,fsg->fs", block_real, sine_part, precision=highest
        )
        return (totals[0] + back_real, totals[1] + back_imag)

    zeros_start = jnp.zeros((bin_index.shape[0], delays.shape[0]), jnp.float32)
    total_real, total_imag = lax.fori_loop(
        0, scan_count // block_size, add_block, (zeros_start, zeros_start)
    )
    return (total_real.T * steer_scale, total_imag.T * steer_scale)


def on_device_plain(histories, bin_index, delays, map_adjoint):
    groups = lax.axis_size("grp")
    sensors = delays.shape[0] * lax.axis_size("sens")
    steer_scale = 1.0 / math.sqrt(sensors)
    block_rows = histories.shape[1]
    position = lax.axis_index("grp")
    weight = 2.0 * map_adjoint[None, :]
    transform = grouped_transform(position * block_rows, block_rows, bin_index, NT, groups)
    partial_value = jnp.dot(histories, transform, preferred_element_type=jnp.float32)
    spectra = lax.psum_scatter(partial_value, "grp", scatter_dimension=1, tiled=True)
    bin_width = bin_index.shape[0] // groups
    own_bins = lax.dynamic_slice_in_dim(bin_index, position * bin_width, bin_width, 0)
    real_part = spectra[:, :bin_width]
    imag_part = spectra[:, bin_width:]
    steer_real, steer_imag = steer_forward(real_part, imag_part, delays, own_bins, NT, steer_scale)
    steer_real, steer_imag = lax.psum((steer_real, steer_imag), "sens")
    back_real, back_imag = steer_back(
        weight * steer_real, weight * steer_imag, delays, own_bins, NT, steer_scale
    )
    adjoint = jnp.concatenate([back_real, back_imag], 1).astype(jnp.bfloat16)
    result = lax.dot_general(
        lax.all_gather(adjoint, "grp", axis=1, tiled=True),
        transform,
        (((1,), (1,)), ((), ())),
        preferred_element_type=jnp.float32,
    )
    return result.astype(jnp.bfloat16)


MESH = pl.DeviceIdType.MESH
COS_T = (0.9999992216, -19.73898252, 64.92872662, -85.27239701, 58.79403871, -21.07678212)
SIN_T = (6.283055799, -41.33121431, 81.36681529, -74.47800454, 32.78140079)
COS_W = (
    0.9999999892,
    -19.73920453,
    64.93911898,
    -85.45016555,
    60.16783172,
    -25.96831327,
    6.529610372,
)
CHUNK = 256


def horner(coefficients, u):
    value = coefficients[-1] * u + coefficients[-2]
    for coefficient in coefficients[-3::-1]:
        value = value * u + coefficient
    return value


def wrapped(turns):
    return turns - jnp.round(turns)


def kernel(
    ns,
    ng,
    scale,
    bins_hbm,
    map_hbm,
    hist_hbm,
    delays_hbm,
    out_ref,
    bins_ref,
    map_own,
    hist,
    delays,
    wave,
    steer,
    spec_out,
    spec_in,
    part_out,
    part_in,
    bar_out,
    bar_in,
    adj,
    local_sem,
    spec_send,
    spec_recv,
    part_send,
    part_recv,
    bar_send,
    bar_recv,
    adj_send,
    adj_recv,
):
    f32, bf16 = jnp.float32, jnp.bfloat16
    sens, grp = lax.axis_index("sens"), lax.axis_index("grp")
    rows, times = hist.shape
    points = delays.shape[1]
    width = points // ns
    half = width // 2
    blocks = wave.shape[0] // 16
    length = times * ng

    def sens_at(offset):
        return lax.rem(sens + offset, ns)

    def grp_at(offset):
        return lax.rem(grp + offset, ng)

    hist_copy = pltpu.make_async_copy(hist_hbm, hist, local_sem.at[0])
    delays_copy = pltpu.make_async_copy(delays_hbm, delays, local_sem.at[1])
    bins_copy = pltpu.make_async_copy(bins_hbm, bins_ref, local_sem.at[2])
    map_at = pl.ds(pl.multiple_of(sens * width, width), width)
    map_copy = pltpu.make_async_copy(map_hbm.at[:, map_at], map_own, local_sem.at[3])
    bins_copy.start()
    hist_copy.start()
    delays_copy.start()
    map_copy.start()
    barrier = pltpu.get_barrier_semaphore()
    for k in range(1, ns):
        pl.semaphore_signal(barrier, inc=1, device_id={"sens": sens_at(k)}, device_id_type=MESH)
    for k in range(1, ng):
        pl.semaphore_signal(barrier, inc=1, device_id={"grp": grp_at(k)}, device_id_type=MESH)

    row8 = lax.broadcasted_iota(jnp.int32, (8, times), 0)
    sample = (grp * times + lax.broadcasted_iota(jnp.int32, (8, times), 1)).astype(f32)
    lower = row8 >= 4
    which = lax.rem(row8, 4)
    bins_copy.wait()
    for j in range(blocks):
        b = [bins_ref[4 * j + i].astype(f32) * (1.0 / length) for i in range(4)]
        column = jnp.where(
            which == 0, b[0], jnp.where(which == 1, b[1], jnp.where(which == 2, b[2], b[3]))
        )
        r = wrapped(sample * column + jnp.where(lower, 0.25, 0.0))
        values = horner(COS_W, r * r) * (1.0 / math.sqrt(length))
        wave[16 * j : 16 * j + 16, :] = jnp.concatenate(
            [values, jnp.zeros((8, times), f32)], 0
        ).astype(bf16)

    hist_copy.wait()
    partial_spectra = lax.dot_general(
        wave[...], hist[...], (((1,), (1,)), ((), ())), preferred_element_type=f32
    )
    spec_out[...] = jnp.zeros(spec_out.shape, f32)
    for j in range(ng):
        spec_out[j, :, 0:rows] = partial_spectra[16 * j : 16 * j + 8, :]
    pl.semaphore_wait(barrier, ns - 1 + ng - 1)

    spec_copies = []
    for k in range(1, ng):
        copy = pltpu.make_async_remote_copy(
            src_ref=spec_out.at[grp_at(k)],
            dst_ref=spec_in.at[k - 1],
            send_sem=spec_send.at[k - 1],
            recv_sem=spec_recv.at[k - 1],
            device_id={"grp": grp_at(k)},
            device_id_type=MESH,
        )
        copy.start()
        spec_copies.append(copy)

    delays_copy.wait()
    own_bins = [bins_ref[4 * grp + i].astype(f32) * (1.0 / length) for i in range(4)]

    def steer_chunk(index, carry):
        at = pl.ds(pl.multiple_of(index * CHUNK, CHUNK), CHUNK)
        delay = delays[:, at].astype(f32)
        for i in range(4):
            r = wrapped(delay * own_bins[i])
            u = r * r
            steer[64 * i : 64 * i + 32, at] = horner(COS_T, u).astype(bf16)
            steer[64 * i + 32 : 64 * i + 64, at] = (horner(SIN_T, u) * r).astype(bf16)
        return carry

    lax.fori_loop(0, points // CHUNK, steer_chunk, 0)

    sign = jnp.where(lax.broadcasted_iota(jnp.int32, (8, 128), 0) < 4, -1.0, 1.0).astype(f32)
    own_block = lax.rem(lax.broadcasted_iota(jnp.int32, (8, 256), 0), 4) == (
        lax.broadcasted_iota(jnp.int32, (8, 256), 1) // 64
    )
    total = spec_out[grp]
    for k in range(1, ng):
        spec_copies[k - 1].wait_recv()
        total = total + spec_in[k - 1]
    both = total + pltpu.roll(sign * pltpu.roll(total, 4, 0), 32, 1)
    both = both + pltpu.roll(both, 64, 1)
    spread = jnp.where(own_block, jnp.concatenate([both, both], 1), 0.0)
    high = spread.astype(bf16).astype(f32)
    lhs = jnp.concatenate([high, spread - high], 0).astype(bf16)

    def steered_part(owner):
        at = pl.ds(pl.multiple_of(owner * width, width), width)
        product = jnp.dot(lhs, steer[:, at], preferred_element_type=f32)
        product = product[0:8] + product[8:16]
        return jnp.concatenate([product[:, 0:half], product[:, half:width]], 0)

    part_copies = []
    for k in range(1, ns):
        part_out[k - 1] = steered_part(sens_at(k)).astype(bf16)
        copy = pltpu.make_async_remote_copy(
            src_ref=part_out.at[k - 1],
            dst_ref=part_in.at[k - 1],
            send_sem=part_send.at[k - 1],
            recv_sem=part_recv.at[k - 1],
            device_id={"sens": sens_at(k)},
            device_id_type=MESH,
        )
        copy.start()
        part_copies.append(copy)
    total = steered_part(sens)
    map_copy.wait()
    first = map_own[:, 0:half]
    second = map_own[:, half:width]
    weight = (2.0 * scale * scale) * jnp.concatenate(
        [jnp.broadcast_to(first, (8, half)), jnp.broadcast_to(second, (8, half))], 0
    )
    for k in range(1, ns):
        part_copies[k - 1].wait_recv()
        total = total + part_in[k - 1].astype(f32)
    bar = (weight * total).astype(bf16)
    bar_out[...] = bar

    bar_copies = []
    for k in range(1, ns):
        copy = pltpu.make_async_remote_copy(
            src_ref=bar_out,
            dst_ref=bar_in.at[k - 1],
            send_sem=bar_send.at[k - 1],
            recv_sem=bar_recv.at[k - 1],
            device_id={"sens": sens_at(k)},
            device_id_type=MESH,
        )
        copy.start()
        bar_copies.append(copy)

    def back_part(values, owner):
        sides = []
        for side in range(2):
            at = pl.ds(pl.multiple_of(owner * width + side * half, half), half)
            sides.append(
                lax.dot_general(
                    values,
                    steer[:, at],
                    (((1,), (1,)), ((), ())),
                    preferred_element_type=f32,
                )
            )
        return sides[0][0:8] + sides[1][8:16]

    back = back_part(bar, sens)
    for k in range(1, ns):
        bar_copies[k - 1].wait_recv()
        back = back + back_part(bar_in[k - 1], sens_at(ns - k))
    back = jnp.where(own_block, back, 0.0)
    back = back[:, 0:128] + back[:, 128:256]
    back = back + pltpu.roll(back, 64, 1)
    back = back - sign * pltpu.roll(pltpu.roll(back, 4, 0), 96, 1)
    own_rows = jnp.concatenate([back, jnp.zeros((8, 128), f32)], 0).astype(bf16)
    adj[grp] = own_rows

    adj_copies = []
    for k in range(1, ng):
        copy = pltpu.make_async_remote_copy(
            src_ref=adj.at[grp],
            dst_ref=adj.at[grp],
            send_sem=adj_send.at[k - 1],
            recv_sem=adj_recv.at[k - 1],
            device_id={"grp": grp_at(k)},
            device_id_type=MESH,
        )
        copy.start()
        adj_copies.append(copy)
    for copy in adj_copies:
        copy.wait_recv()
    gathered = jnp.concatenate([adj[j] for j in range(ng)], 0)
    out_ref[...] = lax.dot_general(
        gathered[:, 0:rows], wave[...], (((0,), (0,)), ((), ())), preferred_element_type=f32
    ).astype(bf16)
    for copy in spec_copies + part_copies + bar_copies + adj_copies:
        copy.wait_send()


def on_device_fused(ns, ng, histories, bin_index, delays, map_adjoint):
    rows, times = histories.shape
    points = delays.shape[1]
    half = points // ns // 2
    dma = pltpu.SemaphoreType.DMA
    vmem = pltpu.VMEM
    return pl.pallas_call(
        functools.partial(kernel, ns, ng, 1.0 / math.sqrt(rows * ns)),
        out_shape=jax.ShapeDtypeStruct((rows, times), jnp.bfloat16),
        in_specs=[
            pl.BlockSpec(memory_space=pltpu.HBM),
            pl.BlockSpec(memory_space=pltpu.HBM),
            pl.BlockSpec(memory_space=pltpu.HBM),
            pl.BlockSpec(memory_space=pltpu.HBM),
        ],
        out_specs=pl.BlockSpec(memory_space=pltpu.VMEM),
        scratch_shapes=[
            pltpu.SMEM((bin_index.shape[0],), jnp.int32),
            vmem((1, 2 * half), jnp.float32),
            vmem((rows, times), jnp.bfloat16),
            vmem((rows, points), jnp.int32),
            vmem((16 * ng, times), jnp.bfloat16),
            vmem((256, points), jnp.bfloat16),
            vmem((ng, 8, 128), jnp.float32),
            vmem((ng - 1, 8, 128), jnp.float32),
            vmem((ns - 1, 16, half), jnp.bfloat16),
            vmem((ns - 1, 16, half), jnp.bfloat16),
            vmem((16, half), jnp.bfloat16),
            vmem((ns - 1, 16, half), jnp.bfloat16),
            vmem((ng, 16, 128), jnp.bfloat16),
            dma((4,)),
            dma((ng - 1,)),
            dma((ng - 1,)),
            dma((ns - 1,)),
            dma((ns - 1,)),
            dma((ns - 1,)),
            dma((ns - 1,)),
            dma((ng - 1,)),
            dma((ng - 1,)),
        ],
        compiler_params=pltpu.CompilerParams(
            collective_id=0, has_side_effects=True, vmem_limit_bytes=64 * 1024 * 1024
        ),
    )(bin_index, map_adjoint.reshape(1, points), histories, delays)


def solution(mesh):
    ns, ng = mesh.shape["sens"], mesh.shape["grp"]
    placed = (P("sens", "grp"), P(), P("sens", None), P())

    def on_device(histories, bin_index, delays, map_adjoint):
        rows, points = delays.shape
        fits = (
            rows == 32
            and bin_index.shape[0] == 4 * ng
            and points % (256 * ns) == 0
            and histories.shape[1] * ng == NT
        )
        if fits:
            return on_device_fused(ns, ng, histories, bin_index, delays, map_adjoint)
        return on_device_plain(histories, bin_index, delays, map_adjoint)

    return jax.shard_map(
        on_device, mesh=mesh, in_specs=placed, out_specs=P("sens", "grp"), check_vma=False
    )
```

```python
import functools
import math

import jax
import jax.numpy as jnp
from jax import lax
from jax.experimental import pallas as pl
from jax.experimental.pallas import tpu as pltpu
from jax.sharding import PartitionSpec as P

NT = 4096


two_pi = 2.0 * math.pi


def grouped_transform(first_sample, sample_count, bin_index, length, groups):
    sample_times = first_sample + lax.iota(jnp.int32, sample_count)
    phase_index = sample_times[:, None] * bin_index[None, :] % length
    phase_angle = phase_index.astype(jnp.float32) * (two_pi / length)
    factor = 1.0 / math.sqrt(length)
    bin_width = bin_index.shape[0] // groups
    cosine = (jnp.cos(phase_angle) * factor).reshape(sample_count, groups, 1, bin_width)
    sine_part = (-jnp.sin(phase_angle) * factor).reshape(sample_count, groups, 1, bin_width)
    joined_parts = jnp.concatenate([cosine, sine_part], 2)
    return joined_parts.reshape(sample_count, 2 * bin_index.shape[0]).astype(jnp.bfloat16)


def angles(bin_index, delay_block, length):
    phase_index = bin_index[:, None, None] * delay_block[None, :, :] % length
    return phase_index.astype(jnp.float32) * (two_pi / length)


def steer_forward(real_part, imag_part, delays, bin_index, length, steer_scale):
    scan_count = delays.shape[1]
    block_size = math.gcd(scan_count, 512)
    real_trans = real_part.T
    imag_trans = imag_part.T
    highest = lax.Precision.HIGHEST

    def one_block(block_index):
        delay_block = lax.dynamic_slice_in_dim(delays, block_index * block_size, block_size, 1)
        phase_angle = angles(bin_index, delay_block, length)
        cosine = jnp.cos(phase_angle)
        sine_part = jnp.sin(phase_angle)
        steer_real = jnp.einsum("fs,fsg->fg", real_trans, cosine, precision=highest) - jnp.einsum(
            "fs,fsg->fg", imag_trans, sine_part, precision=highest
        )
        steer_imag = jnp.einsum(
            "fs,fsg->fg", real_trans, sine_part, precision=highest
        ) + jnp.einsum("fs,fsg->fg", imag_trans, cosine, precision=highest)
        return (steer_real * steer_scale, steer_imag * steer_scale)

    blocks_real, blocks_imag = lax.map(
        one_block, jnp.arange(scan_count // block_size, dtype=jnp.int32)
    )
    bin_count = bin_index.shape[0]
    return (
        blocks_real.transpose(1, 0, 2).reshape(bin_count, scan_count),
        blocks_imag.transpose(1, 0, 2).reshape(bin_count, scan_count),
    )


def steer_back(bar_real, bar_imag, delays, bin_index, length, steer_scale):
    scan_count = delays.shape[1]
    block_size = math.gcd(scan_count, 512)
    highest = lax.Precision.HIGHEST

    def add_block(block_index, totals):
        delay_block = lax.dynamic_slice_in_dim(delays, block_index * block_size, block_size, 1)
        block_real = lax.dynamic_slice_in_dim(bar_real, block_index * block_size, block_size, 1)
        block_imag = lax.dynamic_slice_in_dim(bar_imag, block_index * block_size, block_size, 1)
        phase_angle = angles(bin_index, delay_block, length)
        cosine = jnp.cos(phase_angle)
        sine_part = jnp.sin(phase_angle)
        back_real = jnp.einsum("fg,fsg->fs", block_real, cosine, precision=highest) + jnp.einsum(
            "fg,fsg->fs", block_imag, sine_part, precision=highest
        )
        back_imag = jnp.einsum("fg,fsg->fs", block_imag, cosine, precision=highest) - jnp.einsum(
            "fg,fsg->fs", block_real, sine_part, precision=highest
        )
        return (totals[0] + back_real, totals[1] + back_imag)

    zeros_start = jnp.zeros((bin_index.shape[0], delays.shape[0]), jnp.float32)
    total_real, total_imag = lax.fori_loop(
        0, scan_count // block_size, add_block, (zeros_start, zeros_start)
    )
    return (total_real.T * steer_scale, total_imag.T * steer_scale)


def on_device_plain(histories, bin_index, delays, map_adjoint):
    groups = lax.axis_size("grp")
    sensors = delays.shape[0] * lax.axis_size("sens")
    steer_scale = 1.0 / math.sqrt(sensors)
    block_rows = histories.shape[1]
    position = lax.axis_index("grp")
    weight = 2.0 * map_adjoint[None, :]
    transform = grouped_transform(position * block_rows, block_rows, bin_index, NT, groups)
    partial_value = jnp.dot(histories, transform, preferred_element_type=jnp.float32)
    spectra = lax.psum_scatter(partial_value, "grp", scatter_dimension=1, tiled=True)
    bin_width = bin_index.shape[0] // groups
    own_bins = lax.dynamic_slice_in_dim(bin_index, position * bin_width, bin_width, 0)
    real_part = spectra[:, :bin_width]
    imag_part = spectra[:, bin_width:]
    steer_real, steer_imag = steer_forward(real_part, imag_part, delays, own_bins, NT, steer_scale)
    steer_real, steer_imag = lax.psum((steer_real, steer_imag), "sens")
    back_real, back_imag = steer_back(
        weight * steer_real, weight * steer_imag, delays, own_bins, NT, steer_scale
    )
    adjoint = jnp.concatenate([back_real, back_imag], 1).astype(jnp.bfloat16)
    result = lax.dot_general(
        lax.all_gather(adjoint, "grp", axis=1, tiled=True),
        transform,
        (((1,), (1,)), ((), ())),
        preferred_element_type=jnp.float32,
    )
    return result.astype(jnp.bfloat16)


MESH = pl.DeviceIdType.MESH
COS_T = (0.9999992216, -19.73898252, 64.92872662, -85.27239701, 58.79403871, -21.07678212)
SIN_T = (6.283055799, -41.33121431, 81.36681529, -74.47800454, 32.78140079)
COS_W = (
    0.9999999892,
    -19.73920453,
    64.93911898,
    -85.45016555,
    60.16783172,
    -25.96831327,
    6.529610372,
)
CHUNK = 256


def horner(coefficients, u):
    value = coefficients[-1] * u + coefficients[-2]
    for coefficient in coefficients[-3::-1]:
        value = value * u + coefficient
    return value


def wrapped(turns):
    return turns - jnp.round(turns)


def kernel(
    ns,
    ng,
    scale,
    bins_hbm,
    map_hbm,
    hist_hbm,
    delays_hbm,
    out_ref,
    bins_ref,
    map_own,
    hist,
    delays,
    wave,
    steer,
    spec_out,
    spec_in,
    part_out,
    part_in,
    part_sum,
    bar_in,
    adj,
    local_sem,
    spec_send,
    spec_recv,
    part_send,
    part_recv,
    bar_send,
    bar_recv,
    adj_send,
    adj_recv,
):
    f32, bf16 = jnp.float32, jnp.bfloat16
    sens, grp = lax.axis_index("sens"), lax.axis_index("grp")
    rows, times = hist.shape
    points = delays.shape[1]
    width = points // ns
    half = width // 2
    blocks = wave.shape[0] // 16
    length = times * ng

    def sens_at(offset):
        if ns != 8:
            return lax.rem(sens + offset, ns)
        plane = lax.rem(sens // 4 + offset // 4, 2)
        pair = lax.rem(sens // 2 + offset // 2, 2)
        return 4 * plane + 2 * pair + lax.rem(sens + offset, 2)

    order = list(range(ns - 1, 0, -1))

    def grp_at(offset):
        return lax.rem(grp + offset, ng)

    hist_copy = pltpu.make_async_copy(hist_hbm, hist, local_sem.at[0])
    delays_copy = pltpu.make_async_copy(delays_hbm, delays, local_sem.at[1])
    bins_copy = pltpu.make_async_copy(bins_hbm, bins_ref, local_sem.at[2])
    map_at = pl.ds(pl.multiple_of(sens * width, width), width)
    map_copy = pltpu.make_async_copy(map_hbm.at[:, map_at], map_own, local_sem.at[3])
    bins_copy.start()
    hist_copy.start()
    delays_copy.start()
    map_copy.start()
    barrier = pltpu.get_barrier_semaphore()
    for k in range(1, ns):
        pl.semaphore_signal(barrier, inc=1, device_id={"sens": sens_at(k)}, device_id_type=MESH)
    for k in range(1, ng):
        pl.semaphore_signal(barrier, inc=1, device_id={"grp": grp_at(k)}, device_id_type=MESH)

    row8 = lax.broadcasted_iota(jnp.int32, (8, times), 0)
    sample = (grp * times + lax.broadcasted_iota(jnp.int32, (8, times), 1)).astype(f32)
    lower = row8 >= 4
    which = lax.rem(row8, 4)
    bins_copy.wait()
    for j in range(blocks):
        b = [bins_ref[4 * j + i].astype(f32) * (1.0 / length) for i in range(4)]
        column = jnp.where(
            which == 0, b[0], jnp.where(which == 1, b[1], jnp.where(which == 2, b[2], b[3]))
        )
        r = wrapped(sample * column + jnp.where(lower, 0.25, 0.0))
        values = horner(COS_W, r * r) * (1.0 / math.sqrt(length))
        wave[16 * j : 16 * j + 16, :] = jnp.concatenate(
            [values, jnp.zeros((8, times), f32)], 0
        ).astype(bf16)

    hist_copy.wait()
    partial_spectra = lax.dot_general(
        wave[...], hist[...], (((1,), (1,)), ((), ())), preferred_element_type=f32
    )
    spec_out[...] = jnp.zeros(spec_out.shape, f32)
    for j in range(ng):
        spec_out[j, :, 0:rows] = partial_spectra[16 * j : 16 * j + 8, :]
    pl.semaphore_wait(barrier, ns - 1 + ng - 1)

    spec_copies = []
    for k in range(1, ng):
        copy = pltpu.make_async_remote_copy(
            src_ref=spec_out.at[grp_at(k)],
            dst_ref=spec_in.at[k - 1],
            send_sem=spec_send.at[k - 1],
            recv_sem=spec_recv.at[k - 1],
            device_id={"grp": grp_at(k)},
            device_id_type=MESH,
        )
        copy.start()
        spec_copies.append(copy)

    delays_copy.wait()
    own_bins = [bins_ref[4 * grp + i].astype(f32) * (1.0 / length) for i in range(4)]

    def steer_chunk(index, carry):
        at = pl.ds(pl.multiple_of(index * CHUNK, CHUNK), CHUNK)
        delay = delays[:, at].astype(f32)
        for i in range(4):
            r = wrapped(delay * own_bins[i])
            u = r * r
            steer[64 * i : 64 * i + 32, at] = horner(COS_T, u).astype(bf16)
            steer[64 * i + 32 : 64 * i + 64, at] = (horner(SIN_T, u) * r).astype(bf16)
        return carry

    lax.fori_loop(0, points // CHUNK, steer_chunk, 0)

    sign = jnp.where(lax.broadcasted_iota(jnp.int32, (8, 128), 0) < 4, -1.0, 1.0).astype(f32)
    own_block = lax.rem(lax.broadcasted_iota(jnp.int32, (8, 256), 0), 4) == (
        lax.broadcasted_iota(jnp.int32, (8, 256), 1) // 64
    )
    total = spec_out[grp]
    for k in range(1, ng):
        spec_copies[k - 1].wait_recv()
        total = total + spec_in[k - 1]
    both = total + pltpu.roll(sign * pltpu.roll(total, 4, 0), 32, 1)
    both = both + pltpu.roll(both, 64, 1)
    spread = jnp.where(own_block, jnp.concatenate([both, both], 1), 0.0)
    high = spread.astype(bf16).astype(f32)
    lhs = jnp.concatenate([high, spread - high], 0).astype(bf16)

    for owner in range(ns):
        at = slice(owner * width, (owner + 1) * width)
        product = jnp.dot(lhs, steer[:, at], preferred_element_type=f32)
        product = product[0:8] + product[8:16]
        product = jnp.concatenate([product[:, 0:half], product[:, half:width]], 0)
        part_sum[owner] = product
        part_out[owner] = product.astype(bf16)

    part_copies = []
    for k in order:
        copy = pltpu.make_async_remote_copy(
            src_ref=part_out.at[sens_at(k)],
            dst_ref=part_in.at[k - 1],
            send_sem=part_send.at[k - 1],
            recv_sem=part_recv.at[k - 1],
            device_id={"sens": sens_at(k)},
            device_id_type=MESH,
        )
        copy.start()
        part_copies.append(copy)
    total = part_sum[sens]
    map_copy.wait()
    first = map_own[:, 0:half]
    second = map_own[:, half:width]
    weight = (2.0 * scale * scale) * jnp.concatenate(
        [jnp.broadcast_to(first, (8, half)), jnp.broadcast_to(second, (8, half))], 0
    )
    for copy in part_copies:
        copy.wait_recv()
    for k in range(1, ns):
        total = total + part_in[k - 1].astype(f32)
    bar_in[sens] = (weight * total).astype(bf16)

    bar_copies = []
    for k in order:
        copy = pltpu.make_async_remote_copy(
            src_ref=bar_in.at[sens],
            dst_ref=bar_in.at[sens],
            send_sem=bar_send.at[k - 1],
            recv_sem=bar_recv.at[k - 1],
            device_id={"sens": sens_at(k)},
            device_id_type=MESH,
        )
        copy.start()
        bar_copies.append(copy)

    for copy in bar_copies:
        copy.wait_recv()
    sides = [jnp.zeros((16, 256), f32)] * 2
    for owner in range(ns):
        for side in range(2):
            start = owner * width + side * half
            sides[side] = sides[side] + lax.dot_general(
                bar_in[owner],
                steer[:, start : start + half],
                (((1,), (1,)), ((), ())),
                preferred_element_type=f32,
            )
    back = sides[0][0:8] + sides[1][8:16]
    back = jnp.where(own_block, back, 0.0)
    back = back[:, 0:128] + back[:, 128:256]
    back = back + pltpu.roll(back, 64, 1)
    back = back - sign * pltpu.roll(pltpu.roll(back, 4, 0), 96, 1)
    own_rows = jnp.concatenate([back, jnp.zeros((8, 128), f32)], 0).astype(bf16)
    adj[grp] = own_rows

    adj_copies = []
    for k in range(1, ng):
        copy = pltpu.make_async_remote_copy(
            src_ref=adj.at[grp],
            dst_ref=adj.at[grp],
            send_sem=adj_send.at[k - 1],
            recv_sem=adj_recv.at[k - 1],
            device_id={"grp": grp_at(k)},
            device_id_type=MESH,
        )
        copy.start()
        adj_copies.append(copy)
    for copy in adj_copies:
        copy.wait_recv()
    gathered = jnp.concatenate([adj[j] for j in range(ng)], 0)
    out_ref[...] = lax.dot_general(
        gathered[:, 0:rows], wave[...], (((0,), (0,)), ((), ())), preferred_element_type=f32
    ).astype(bf16)
    for copy in spec_copies + part_copies + bar_copies + adj_copies:
        copy.wait_send()


def on_device_fused(ns, ng, histories, bin_index, delays, map_adjoint):
    rows, times = histories.shape
    points = delays.shape[1]
    half = points // ns // 2
    dma = pltpu.SemaphoreType.DMA
    vmem = pltpu.VMEM
    return pl.pallas_call(
        functools.partial(kernel, ns, ng, 1.0 / math.sqrt(rows * ns)),
        out_shape=jax.ShapeDtypeStruct((rows, times), jnp.bfloat16),
        in_specs=[
            pl.BlockSpec(memory_space=pltpu.HBM),
            pl.BlockSpec(memory_space=pltpu.HBM),
            pl.BlockSpec(memory_space=pltpu.HBM),
            pl.BlockSpec(memory_space=pltpu.HBM),
        ],
        out_specs=pl.BlockSpec(memory_space=pltpu.VMEM),
        scratch_shapes=[
            pltpu.SMEM((bin_index.shape[0],), jnp.int32),
            vmem((1, 2 * half), jnp.float32),
            vmem((rows, times), jnp.bfloat16),
            vmem((rows, points), jnp.int32),
            vmem((16 * ng, times), jnp.bfloat16),
            vmem((256, points), jnp.bfloat16),
            vmem((ng, 8, 128), jnp.float32),
            vmem((ng - 1, 8, 128), jnp.float32),
            vmem((ns, 16, half), jnp.bfloat16),
            vmem((ns - 1, 16, half), jnp.bfloat16),
            vmem((ns, 16, half), jnp.float32),
            vmem((ns, 16, half), jnp.bfloat16),
            vmem((ng, 16, 128), jnp.bfloat16),
            dma((4,)),
            dma((ng - 1,)),
            dma((ng - 1,)),
            dma((ns - 1,)),
            dma((ns - 1,)),
            dma((ns - 1,)),
            dma((ns - 1,)),
            dma((ng - 1,)),
            dma((ng - 1,)),
        ],
        compiler_params=pltpu.CompilerParams(
            collective_id=0, has_side_effects=True, vmem_limit_bytes=64 * 1024 * 1024
        ),
    )(bin_index, map_adjoint.reshape(1, points), histories, delays)


def solution(mesh):
    ns, ng = mesh.shape["sens"], mesh.shape["grp"]
    placed = (P("sens", "grp"), P(), P("sens", None), P())

    def on_device(histories, bin_index, delays, map_adjoint):
        rows, points = delays.shape
        fits = (
            rows == 32
            and bin_index.shape[0] == 4 * ng
            and points % (256 * ns) == 0
            and histories.shape[1] * ng == NT
        )
        if fits:
            return on_device_fused(ns, ng, histories, bin_index, delays, map_adjoint)
        return on_device_plain(histories, bin_index, delays, map_adjoint)

    return jax.shard_map(
        on_device, mesh=mesh, in_specs=placed, out_specs=P("sens", "grp"), check_vma=False
    )
```
